256 devices in a mesh: sample: 16 (over z_lo, x), expert: 16 (over y, z_hi, core).
Axes of the slice: x: 4, y: 4, z: 8 (z_hi: 2, z_lo: 4; z = z_hi * 4 + z_lo), core: 2. Of those that a mesh axis runs over, the one named last changes fastest.
Arguments:
- prompt_input: bfloat16 [16, 16, 64, 2048], P('expert', 'sample'), may hold values from -6 to 6
- prompt_query: bfloat16 [16, 16, 64, 2048], P('expert', 'sample'), may hold values from -6 to 6
- prompt_key: bfloat16 [16, 16, 64, 2048], P('expert', 'sample'), may hold values from -6 to 6
- prompt_value: bfloat16 [16, 16, 64, 2048], P('expert', 'sample'), may hold values from -6 to 6
- prompt_gate: bfloat16 [16, 16, 64, 2048], P('expert', 'sample'), may hold values from -6 to 6
- prompt_beta: bfloat16 [16, 16, 64, 16], P('expert', 'sample'), may hold values from 0.099609375 to 0.8984375
- prompt_decay: bfloat16 [16, 16, 64, 16], P('expert', 'sample'), may hold values from -1 to 0, as said below
- prompt_routes: int32 [16, 16, 64, 10], P('expert', 'sample'), may hold values from 0 to 15, all different within a row; in each aligned block of 64 rows (0 to 63, 64 to 127, ..., all dimensions but the last counted through in order) at most 42 rows name the same one
- prompt_weights: float32 [16, 16, 64, 10], P('expert', 'sample'), may hold values from 0.05 to 0.3
- sample_input: bfloat16 [4, 16, 16, 16, 2048], P(None, 'sample', 'expert'), may hold values from -6 to 6
- sample_query: bfloat16 [4, 16, 16, 16, 2048], P(None, 'sample', 'expert'), may hold values from -6 to 6
- sample_key: bfloat16 [4, 16, 16, 16, 2048], P(None, 'sample', 'expert'), may hold values from -6 to 6
- sample_value: bfloat16 [4, 16, 16, 16, 2048], P(None, 'sample', 'expert'), may hold values from -6 to 6
- sample_gate: bfloat16 [4, 16, 16, 16, 2048], P(None, 'sample', 'expert'), may hold values from -6 to 6
- sample_beta: bfloat16 [4, 16, 16, 16, 16], P(None, 'sample', 'expert'), may hold values from 0.099609375 to 0.8984375
- sample_decay: bfloat16 [4, 16, 16, 16, 16], P(None, 'sample', 'expert'), may hold values from -1 to 0, as said below
- sample_routes: int32 [4, 16, 16, 16, 10], P(None, 'sample', 'expert'), may hold values from 0 to 15, all different within a row; in each aligned block of 16 rows (0 to 15, 16 to 31, ..., all dimensions but the last counted through in order) at most 11 rows name the same one
- sample_weights: float32 [4, 16, 16, 16, 10], P(None, 'sample', 'expert'), may hold values from 0.05 to 0.3
- head_gain: float32 [128], replicated, may hold values from 0.25 to 1.75
- norm_gain: float32 [2048], replicated, may hold values from 0.25 to 1.75
- expert_gate: bfloat16 [16, 2048, 512], P('expert'), may hold values from -0.125 to 0.125
- expert_up: bfloat16 [16, 2048, 512], P('expert'), may hold values from -0.125 to 0.125
- expert_down: bfloat16 [16, 512, 2048], P('expert'), may hold values from -0.25 to 0.25
Outputs:
- prompt_output: bfloat16 [16, 16, 64, 2048], P('expert', 'sample')
- sample_output: bfloat16 [4, 16, 16, 16, 2048], P(None, 'sample', 'expert')
The draws below stay inside these ranges and needn't reach their ends.
Inputs may be any that keep to these rules, and one draw needn't show every extreme that they name: `prompt_routes`: each row names 10 different experts; among the 64 rows of one device (aligned blocks) no expert is named more than 42 times, a bound that some block reaches. `sample_routes`: each row names 10 different experts; among the 16 rows of one device and step (aligned blocks) no expert is named more than 11 times, a bound that some block reaches. `prompt_decay`: every entry is negative. `sample_decay`: every entry is negative.
All inputs are finite; a program needn't handle non-finite values.
Results may differ from the reference program's by a relative error of at most 0.012.
Values may be sent and summed in bfloat16 or wider, within the bound.
A program may use at most 128 MiB of HBM per device.

```python
import math
import jax
import jax.numpy as jnp
import numpy as np
from jax import lax

D = 2048
HEADS = 16
HEAD_DIM = 128
EXPERT_FF = 512
TOP = 10
EXPERTS = 16
PROMPT_LEN = 64
BLOCK = 32
STEPS = 4
SAMPLES = 16
CAP = 42
DCAP = 11
N_EXPERT = 16


def head_rates(key, low_log, high_log):
    spread = jax.random.uniform(jax.random.fold_in(key, 101), (HEADS,), jnp.float32)
    return jnp.exp(low_log + spread * (high_log - low_log))


def decay_field(key, forgetting_rates, outer_dimensions, vary_shape):
    first, second, final_segment, fourth = jax.random.split(key, 4)
    accelerator_factor = jnp.exp(jax.random.uniform(first, vary_shape, jnp.float32, math.log(0.5), math.log(2.0)))
    rough_guess = jax.random.uniform(second, outer_dimensions + (HEADS,), jnp.float32, 0.5, 1.5)
    sudden_jumps = jax.random.bernoulli(final_segment, 0.03, outer_dimensions + (1,)).astype(jnp.float32)
    input_magnitude = jax.random.uniform(fourth, outer_dimensions + (1,), jnp.float32, 0.22, 0.69)
    return -(forgetting_rates * accelerator_factor * rough_guess) - sudden_jumps * input_magnitude


def draw_prompt_decay(key, part):
    forgetting_rates = head_rates(key, math.log(1.0 / 400.0), math.log(1.0 / 20.0))
    key = jax.random.fold_in(key, 3)
    field = decay_field(key, forgetting_rates, (N_EXPERT, SAMPLES, PROMPT_LEN), (N_EXPERT, SAMPLES, 1, 1))
    return field.astype(jnp.bfloat16)


def draw_sample_decay(key, part):
    forgetting_rates = head_rates(key, math.log(1.0 / 400.0), math.log(1.0 / 20.0))
    key = jax.random.fold_in(key, 5)
    field = decay_field(key, forgetting_rates, (STEPS, SAMPLES, N_EXPERT, SAMPLES), (1, SAMPLES, N_EXPERT, SAMPLES, 1))
    return field.astype(jnp.bfloat16)


def level_of(stream_key, shape, cuts, least, largest):
    def one(dim, parts):
        heights = jax.random.uniform(jax.random.fold_in(jax.random.fold_in(stream_key, 6), dim), (parts,), jnp.float32, least / len(cuts), largest / len(cuts))
        return jnp.repeat(jnp.exp(heights), shape[dim] // parts).reshape((-1,) + (1,) * (len(shape) - dim - 1))

    loudness = one(*cuts[0])
    for cut in cuts[1:]:
        loudness = loudness * one(*cut)
    return loudness


def shared_out(key, own, number, rows, number_of, top, limit, slope):
    ranking = jax.random.permutation(key, number_of)
    heavy_load, common = shares(number_of, rows * top, limit, slope, True), shares(number_of, rows * top, limit, slope, False)
    places = jnp.arange(number_of)

    def named(lengths, turn):
        used = int((lengths > 0).sum())
        fixed = max(1, used // 4)
        shifted = fixed + (places - fixed + turn * (used - fixed)) % max(1, number_of - fixed)
        return jnp.zeros((number_of,), jnp.int32).at[ranking[jnp.where(places < fixed, places, shifted)]].set(jnp.asarray(lengths, jnp.int32))

    lengths = jnp.where(number % 4 == 0, named(heavy_load, number // 4), named(common, number - number // 4 - 1))
    mixed = jax.random.permutation(jax.random.fold_in(own, 3), number_of)
    donor, taker = mixed[0:number_of // 2 * 2:2], mixed[1:number_of // 2 * 2:2]
    margin = jnp.minimum(lengths[donor] - 1, limit - lengths[taker]) // 2
    margin = jnp.where((donor == ranking[0]) | (taker == ranking[0]) | (lengths[taker] == 0), 0, jnp.maximum(margin, 0))
    shifted = jax.random.randint(jax.random.fold_in(own, 4), (number_of // 2,), 0, 1 << 20) % (margin + 1)
    lengths = lengths.at[donor].add(-shifted).at[taker].add(shifted)
    labels = jnp.searchsorted(jnp.cumsum(lengths), jnp.arange(rows * top), side="right").astype(jnp.int32)
    listing = labels.reshape(top, rows).T
    listing = listing[jax.random.permutation(jax.random.fold_in(own, 1), rows)]
    turn = jax.random.randint(jax.random.fold_in(own, 2), (rows, 1), 0, top)
    return jnp.take_along_axis(listing, (jnp.arange(top)[None, :] + turn) % top, axis=1)


def shares(count, total, bound, lean, full):
    loads = [(1 << 20) // math.isqrt(standing ** lean) + 1 for standing in range(1, count + 1)]
    largest = bound if full else min(bound, max(-(-total // count), total * loads[0] // sum(loads)))
    least = 1 if total - largest >= count - 1 else 0
    given, surplus = [largest] + [least] * (count - 1), total - largest - least * (count - 1)
    while surplus > 0:
        free = [i for i in range(1, count) if given[i] < largest] or [i for i in range(1, count) if given[i] < bound]
        whole, budget = sum([loads[i] for i in free]), surplus
        for i in free:
            more = min(bound - given[i], max(1, budget * loads[i] // whole), surplus)
            given[i] = given[i] + more
            surplus = surplus - more
    return np.array(given)


def gaussian(key, dims, scale, bound, shards=(), kind=jnp.bfloat16):
    gain = level_of(key, dims, shards, -0.22, 0.18) if shards else 1.0
    values = jax.random.normal(key, dims, jnp.float32) * scale * gain
    return jnp.minimum(jnp.maximum(values, -bound), bound).astype(kind)


def setup_inputs(seed: int = 0) -> dict:
    splits = jax.random.split(jax.random.key(seed), 24)
    prompt_input = gaussian(splits[0], (N_EXPERT, SAMPLES, PROMPT_LEN, D), 1.0, 6.0, ((0, 16), (1, 16)))
    prompt_query = gaussian(splits[1], (N_EXPERT, SAMPLES, PROMPT_LEN, D), 1.0, 6.0, ((0, 16), (1, 16)))
    prompt_key = gaussian(splits[2], (N_EXPERT, SAMPLES, PROMPT_LEN, D), 1.0, 6.0, ((0, 16), (1, 16)))
    prompt_value = gaussian(splits[3], (N_EXPERT, SAMPLES, PROMPT_LEN, D), 1.0, 6.0, ((0, 16), (1, 16)))
    prompt_gate = gaussian(splits[4], (N_EXPERT, SAMPLES, PROMPT_LEN, D), 1.5, 6.0, ((0, 16), (1, 16)))
    prompt_beta = jnp.clip(0.099609375 + 0.7988281 * jax.random.uniform(splits[5], (N_EXPERT, SAMPLES, PROMPT_LEN, HEADS), jnp.float32) ** level_of(splits[5], (N_EXPERT, SAMPLES, PROMPT_LEN, HEADS), ((0, 16), (1, 16)), -0.2, 0.2), 0.099609375, 0.8984375).astype(jnp.bfloat16)
    prompt_decay = draw_prompt_decay(jax.random.fold_in(splits[23], 71), 0)
    prompt_routes_keys = jax.random.split(jax.random.fold_in(splits[7], 1), N_EXPERT * SAMPLES * PROMPT_LEN // PROMPT_LEN)
    prompt_routes_turns = jax.random.permutation(jax.random.fold_in(splits[7], 3), N_EXPERT * SAMPLES * PROMPT_LEN // PROMPT_LEN)
    prompt_routes = jax.vmap(lambda own, number: shared_out(jax.random.fold_in(splits[7], 2), own, number, PROMPT_LEN, EXPERTS, TOP, CAP, 2))(prompt_routes_keys, prompt_routes_turns).reshape((N_EXPERT, SAMPLES, PROMPT_LEN, TOP))
    prompt_weights = jnp.clip(0.05 + 0.25 * jax.random.uniform(splits[8], (N_EXPERT, SAMPLES, PROMPT_LEN, TOP), jnp.float32) ** level_of(splits[8], (N_EXPERT, SAMPLES, PROMPT_LEN, TOP), ((0, 16), (1, 16)), -0.2, 0.2), 0.05, 0.3)
    sample_input = gaussian(splits[9], (STEPS, SAMPLES, N_EXPERT, SAMPLES, D), 1.0, 6.0, ((1, 16), (2, 16)))
    sample_query = gaussian(splits[10], (STEPS, SAMPLES, N_EXPERT, SAMPLES, D), 1.0, 6.0, ((1, 16), (2, 16)))
    sample_key = gaussian(splits[11], (STEPS, SAMPLES, N_EXPERT, SAMPLES, D), 1.0, 6.0, ((1, 16), (2, 16)))
    sample_value = gaussian(splits[12], (STEPS, SAMPLES, N_EXPERT, SAMPLES, D), 1.0, 6.0, ((1, 16), (2, 16)))
    sample_gate = gaussian(splits[13], (STEPS, SAMPLES, N_EXPERT, SAMPLES, D), 1.5, 6.0, ((1, 16), (2, 16)))
    sample_beta = jnp.clip(0.099609375 + 0.7988281 * jax.random.uniform(splits[14], (STEPS, SAMPLES, N_EXPERT, SAMPLES, HEADS), jnp.float32) ** level_of(splits[14], (STEPS, SAMPLES, N_EXPERT, SAMPLES, HEADS), ((1, 16), (2, 16)), -0.2, 0.2), 0.099609375, 0.8984375).astype(jnp.bfloat16)
    sample_decay = draw_sample_decay(jax.random.fold_in(splits[23], 71), 0)
    sample_routes_keys = jax.random.split(jax.random.fold_in(splits[16], 1), STEPS * SAMPLES * N_EXPERT * SAMPLES // SAMPLES)
    sample_routes_turns = jax.random.permutation(jax.random.fold_in(splits[16], 3), STEPS * SAMPLES * N_EXPERT * SAMPLES // SAMPLES)
    sample_routes = jax.vmap(lambda own, number: shared_out(jax.random.fold_in(splits[16], 2), own, number, SAMPLES, EXPERTS, TOP, DCAP, 2))(sample_routes_keys, sample_routes_turns).reshape((STEPS, SAMPLES, N_EXPERT, SAMPLES, TOP))
    sample_weights = jnp.clip(0.05 + 0.25 * jax.random.uniform(splits[17], (STEPS, SAMPLES, N_EXPERT, SAMPLES, TOP), jnp.float32) ** level_of(splits[17], (STEPS, SAMPLES, N_EXPERT, SAMPLES, TOP), ((1, 16), (2, 16)), -0.2, 0.2), 0.05, 0.3)
    head_gain = jnp.clip(1.0 + 0.15 * jax.random.normal(splits[18], (HEAD_DIM,), jnp.float32), 0.25, 1.75)
    norm_gain = jnp.clip(1.0 + 0.15 * jax.random.normal(splits[19], (D,), jnp.float32), 0.25, 1.75)
    expert_gate = gaussian(splits[20], (EXPERTS, D, EXPERT_FF), D ** -0.5, 0.125, ((0, 16),))
    expert_up = gaussian(splits[21], (EXPERTS, D, EXPERT_FF), D ** -0.5, 0.125, ((0, 16),))
    expert_down = gaussian(splits[22], (EXPERTS, EXPERT_FF, D), EXPERT_FF ** -0.5, 0.25, ((0, 16),))
    return {"prompt_input": prompt_input, "prompt_query": prompt_query, "prompt_key": prompt_key, "prompt_value": prompt_value, "prompt_gate": prompt_gate, "prompt_beta": prompt_beta, "prompt_decay": prompt_decay, "prompt_routes": prompt_routes, "prompt_weights": prompt_weights, "sample_input": sample_input, "sample_query": sample_query, "sample_key": sample_key, "sample_value": sample_value, "sample_gate": sample_gate, "sample_beta": sample_beta, "sample_decay": sample_decay, "sample_routes": sample_routes, "sample_weights": sample_weights, "head_gain": head_gain, "norm_gain": norm_gain, "expert_gate": expert_gate, "expert_up": expert_up, "expert_down": expert_down}


epsilon = 1e-06
highest = lax.Precision.HIGHEST

def split_heads(matrix, head_count):
    return matrix.astype(jnp.float32).reshape(matrix.shape[:-1] + (head_count, matrix.shape[-1] // head_count))

def unit_heads(matrix, head_count):
    parted = split_heads(matrix, head_count)
    return parted * lax.rsqrt(lax.optimization_barrier(jnp.sum(parted * parted, axis=-1, keepdims=True)) + epsilon)

def gated_norm(output_heads, gate_input, head_gain):
    head_count = output_heads.shape[-2]
    scaled = output_heads * lax.rsqrt(lax.optimization_barrier(jnp.mean(output_heads * output_heads, axis=-1, keepdims=True)) + epsilon)
    gated = scaled * head_gain * jax.nn.silu(split_heads(gate_input, head_count))
    return gated.reshape(output_heads.shape[:-2] + (-1,)).astype(jnp.bfloat16)

def rms_norm(residual, norm_gain):
    scaled = residual * lax.rsqrt(lax.optimization_barrier(jnp.mean(residual * residual, axis=-1, keepdims=True)) + epsilon)
    return (scaled * norm_gain).astype(jnp.bfloat16)

def block_update(carry_state, pieces):
    query_unit, key_unit, value_heads, beta_rows, decay_rows = pieces
    block_width = query_unit.shape[0]
    cumulative = jnp.cumsum(decay_rows, axis=0).T
    query_major = jnp.swapaxes(query_unit, 0, 1)
    key_major = jnp.swapaxes(key_unit, 0, 1)
    value_major = jnp.swapaxes(value_heads, 0, 1)
    positions = jnp.arange(block_width, dtype=jnp.int32)
    lower_mask = positions[:, None] >= positions[None, :]
    strict = positions[:, None] > positions[None, :]
    log_gap = cumulative[:, :, None] - cumulative[:, None, :]
    decay_mat = jnp.where(lower_mask, jnp.exp(jnp.where(lower_mask, log_gap, 0.0)), 0.0)
    beta_major = beta_rows.T[:, :, None]
    key_inner = jnp.einsum('htd,hjd->htj', key_major, key_major, precision=highest)
    system = jnp.eye(block_width, dtype=jnp.float32) + jnp.where(strict, beta_major * key_inner * decay_mat, 0.0)
    start_decay = jnp.exp(cumulative)[:, :, None]
    carried = jnp.einsum('htd,hde->hte', key_major, carry_state, precision=highest)
    right_side = beta_major * (value_major - start_decay * carried)
    fresh = lax.linalg.triangular_solve(system, right_side, left_side=True, lower=True, unit_diagonal=True)
    query_inner = jnp.einsum('htd,hjd->htj', query_major, key_major, precision=highest) * decay_mat
    output_heads = start_decay * jnp.einsum('htd,hde->hte', query_major, carry_state, precision=highest)
    output_heads = output_heads + jnp.einsum('htj,hje->hte', query_inner, fresh, precision=highest)
    tail_decay = jnp.exp(cumulative[:, -1:] - cumulative)[:, :, None]
    carry_state = jnp.exp(cumulative[:, -1])[:, None, None] * carry_state
    carry_state = carry_state + jnp.einsum('hjd,hje->hde', key_major * tail_decay, fresh, precision=highest)
    return (carry_state, jnp.swapaxes(output_heads, 0, 1))

def prompt_delta(query_rows, key_rows, value_rows, beta_rows, decay_rows, block_width, head_count):
    query_unit = unit_heads(query_rows, head_count)
    key_unit = unit_heads(key_rows, head_count)
    value_heads = split_heads(value_rows, head_count)
    length = query_rows.shape[0]
    block_count = length // block_width

    def blocked(array):
        return array.reshape((block_count, block_width) + array.shape[1:])
    initial = jnp.zeros((head_count, key_unit.shape[-1], value_heads.shape[-1]), jnp.float32)
    final_state, outputs = lax.scan(block_update, initial, (blocked(query_unit), blocked(key_unit), blocked(value_heads), blocked(beta_rows.astype(jnp.float32)), blocked(decay_rows.astype(jnp.float32))))
    return (final_state, outputs.reshape((length,) + outputs.shape[2:]))

def decode_delta(states, query_steps, key_steps, value_steps, gate_steps, beta_steps, decay_steps, head_gain):
    head_count = states.shape[1]
    results = []
    for position in range(query_steps.shape[0]):
        query_unit = unit_heads(query_steps[position], head_count)
        key_unit = unit_heads(key_steps[position], head_count)
        value_heads = split_heads(value_steps[position], head_count)
        keeping = jnp.exp(decay_steps[position].astype(jnp.float32))[:, :, None]
        recalled = jnp.einsum('rhd,rhde->rhe', key_unit, states, precision=highest)
        fresh = beta_steps[position].astype(jnp.float32)[:, :, None] * (value_heads - keeping * recalled)
        states = keeping[..., None] * states + key_unit[..., :, None] * fresh[..., None, :]
        output_heads = jnp.einsum('rhd,rhde->rhe', query_unit, states, precision=highest)
        results.append(gated_norm(output_heads, gate_steps[position], head_gain))
    return jnp.stack(results)

def expert_mlp(matrix, gate_weight, up_weight, down_weight):
    gate_proj = jnp.dot(matrix.astype(jnp.float32), gate_weight.astype(jnp.float32), preferred_element_type=jnp.float32)
    up_proj = jnp.dot(matrix.astype(jnp.float32), up_weight.astype(jnp.float32), preferred_element_type=jnp.float32)
    hidden = (jax.nn.silu(gate_proj) * up_proj).astype(jnp.bfloat16)
    return jnp.dot(hidden.astype(jnp.float32), down_weight.astype(jnp.float32), preferred_element_type=jnp.float32).astype(jnp.bfloat16)

def routed_sum(row_blocks, route_blocks, weight_blocks, capacity, expert_gate, expert_up, expert_down):
    block_total, per_block, top_count = route_blocks.shape
    width = row_blocks.shape[-1]
    expert_count = expert_gate.shape[0]
    flat_routes = route_blocks.reshape(block_total, per_block * top_count)
    matches = (flat_routes[:, :, None] == jnp.arange(expert_count, dtype=jnp.int32)[None, None, :]).astype(jnp.int32)
    ranked = jnp.cumsum(matches, axis=1) - matches
    slot_index = lax.optimization_barrier(jnp.sum(ranked * matches, axis=2))
    token_index = jnp.broadcast_to(jnp.arange(per_block * top_count, dtype=jnp.int32) // top_count, (block_total, per_block * top_count))
    block_index = jnp.broadcast_to(jnp.arange(block_total, dtype=jnp.int32)[:, None], (block_total, per_block * top_count))
    source = jnp.full((block_total, expert_count, capacity), per_block, jnp.int32).at[block_index, flat_routes, slot_index].set(token_index)
    weight_table = jnp.zeros((block_total, expert_count, capacity), jnp.float32).at[block_index, flat_routes, slot_index].set(weight_blocks.reshape(block_total, -1).astype(jnp.float32))
    padded = jnp.concatenate([row_blocks, jnp.zeros((block_total, 1, width), row_blocks.dtype)], axis=1)
    blocks_col = jnp.arange(block_total, dtype=jnp.int32)[:, None]

    def one_expert(running, pieces):
        source_rows, weight_rows, gate_weight, up_weight, down_weight = pieces
        picked = padded[blocks_col, source_rows]
        produced = expert_mlp(picked.reshape(-1, width), gate_weight, up_weight, down_weight).reshape(block_total, capacity, width)
        running = running.at[blocks_col, source_rows].add(weight_rows[:, :, None] * produced.astype(jnp.float32))
        return (running, None)
    initial = jnp.zeros((block_total, per_block + 1, width), jnp.float32)
    running, _ = lax.scan(one_expert, initial, (jnp.swapaxes(source, 0, 1), jnp.swapaxes(weight_table, 0, 1), expert_gate, expert_up, expert_down))
    return running[:, :per_block]

def reference(prompt_input, prompt_query, prompt_key, prompt_value, prompt_gate, prompt_beta, prompt_decay, prompt_routes, prompt_weights, sample_input, sample_query, sample_key, sample_value, sample_gate, sample_beta, sample_decay, sample_routes, sample_weights, head_gain, norm_gain, expert_gate, expert_up, expert_down):
    prompts = N_EXPERT * SAMPLES

    def flat_prompts(array):
        return array.reshape((prompts,) + array.shape[2:])

    def one_prompt(pieces):
        return prompt_delta(pieces[0], pieces[1], pieces[2], pieces[3], pieces[4], BLOCK, HEADS)
    prompt_state, prompt_mixed = lax.map(one_prompt, (flat_prompts(prompt_query), flat_prompts(prompt_key), flat_prompts(prompt_value), flat_prompts(prompt_beta), flat_prompts(prompt_decay)))
    prompt_attn = gated_norm(prompt_mixed, flat_prompts(prompt_gate), head_gain)
    prompt_resid = flat_prompts(prompt_input).astype(jnp.float32) + prompt_attn.astype(jnp.float32)
    prompt_normed = rms_norm(prompt_resid, norm_gain)
    prompt_routed = routed_sum(prompt_normed, flat_prompts(prompt_routes), flat_prompts(prompt_weights), CAP, expert_gate, expert_up, expert_down)
    prompt_output = (prompt_resid + prompt_routed).astype(jnp.bfloat16).reshape(prompt_input.shape)

    def by_sample(array):
        turned = jnp.swapaxes(array, 0, 1)
        return turned.reshape(turned.shape[:2] + (prompts,) + turned.shape[4:])

    def one_sample(pieces):
        return decode_delta(prompt_state, pieces[0], pieces[1], pieces[2], pieces[3], pieces[4], pieces[5], head_gain)
    sample_attn = lax.map(one_sample, tuple([by_sample(array) for array in (sample_query, sample_key, sample_value, sample_gate, sample_beta, sample_decay)]))
    sample_attn = jnp.swapaxes(sample_attn, 0, 1).reshape(sample_input.shape)
    base_resid = sample_input.astype(jnp.float32) + sample_attn.astype(jnp.float32)
    device_rows = (SAMPLES * N_EXPERT, SAMPLES)
    outputs = []
    for position in range(STEPS):
        step_resid = base_resid[position]
        if position > 0:
            step_resid = step_resid + outputs[-1].astype(jnp.float32)
        step_normed = rms_norm(step_resid, norm_gain)
        step_routed = routed_sum(step_normed.reshape(device_rows + (D,)), sample_routes[position].reshape(device_rows + (TOP,)), sample_weights[position].reshape(device_rows + (TOP,)), DCAP, expert_gate, expert_up, expert_down)
        outputs.append((step_resid + step_routed.reshape(step_resid.shape)).astype(jnp.bfloat16))
    sample_output = jnp.stack(outputs)
    return (prompt_output, sample_output)
```

```python
import functools

import jax
import jax.numpy as jnp
from jax import lax
from jax.experimental import pallas as pl
from jax.experimental.pallas import tpu as pltpu
from jax.sharding import PartitionSpec as P

HEADS = 16
DIM = 2048
FF = 512
TOK = 64
WIDE = DIM + 128
HALF = 1024
EPS = 1e-6
MESH = pl.DeviceIdType.MESH
F32 = jnp.float32
BF16 = jnp.bfloat16


def iota(shape, dim):
    return lax.broadcasted_iota(jnp.int32, shape, dim)


def dot(a, b):
    return jnp.dot(a, b, preferred_element_type=F32)


def dot_nt(a, b):
    return lax.dot_general(a, b, (((1,), (1,)), ((), ())), preferred_element_type=F32)


def dot_tn(a, b):
    return lax.dot_general(a, b, (((0,), (0,)), ((), ())), preferred_element_type=F32)


def silu(x):
    return x / (1.0 + jnp.exp(-x))


def split2(x):
    high = x.astype(BF16).astype(F32)
    return high, x - high


def swap_matrix():
    row, col = iota((256, 256), 0), iota((256, 256), 1)
    return jnp.where((col % 16) * 16 + col // 16 == row, 1.0, 0.0).astype(BF16)


def product3(a, b, left):
    a_high, a_low = split2(a)
    b_high, b_low = split2(b)
    lhs = jnp.concatenate(
        [jnp.where(left, a_high, a_low), jnp.where(left, a_high, 0.0)], axis=1
    ).astype(BF16)
    rhs = jnp.concatenate([b_high, b_high, b_low, jnp.zeros_like(b_low)], axis=0).astype(BF16)
    return dot(lhs, rhs)


def gated(out, gate, gain):
    scaled = out * lax.rsqrt(jnp.mean(out * out, axis=-1, keepdims=True) + EPS)
    return (scaled * gain * silu(gate)).astype(BF16)


def prompt_heads(heads, pq, pk, pv, pg, gain, log_rows, beta_rows, state, pattn):
    row, lane = iota((TOK, 128), 0), iota((TOK, 128), 1)
    left = lane < TOK
    col = lane % TOK
    eye = row == col
    eye_left = eye & left
    lower = row >= col
    strict = row > col
    unit = jnp.where(eye, 1.0, 0.0)

    def to_column(row_vector):
        return jnp.sum(jnp.where(eye_left, row_vector, 0.0), axis=1, keepdims=True)

    work = []
    for head in heads:
        lanes = pl.ds(pl.multiple_of(head * 128, 128), 128)
        query, key = pq[:, lanes], pk[:, lanes]
        keys = jnp.concatenate([key, key], axis=0)
        inner, cross = dot_nt(key, keys), dot_nt(query, keys)
        square_row = jnp.sum(jnp.where(eye, inner, 0.0), axis=0, keepdims=True)
        norm_row = lax.rsqrt(square_row + EPS)
        norm_col = to_column(norm_row)
        query32 = query.astype(F32)
        query_norm = lax.rsqrt(jnp.sum(query32 * query32, axis=-1, keepdims=True) + EPS)
        log_row = log_rows[pl.ds(head, 1), :]
        log_col = to_column(log_row)
        beta_col = to_column(beta_rows[pl.ds(head, 1), :])
        decay = jnp.where(lower, jnp.exp(jnp.where(lower, log_col - log_row, 0.0)), 0.0)
        scaled = decay * norm_row
        system = jnp.where(strict, inner * scaled * (norm_col * beta_col), 0.0)
        attend = cross * scaled * query_norm
        values = pv[:, lanes].astype(F32) * beta_col
        tail = jnp.exp(jnp.sum(jnp.where(row[:, :1] == TOK - 1, log_col, 0.0), axis=0, keepdims=True) - log_col)
        work.append([lanes, key, system, attend, values, tail * norm_col, head])
    firsts = []
    for item in work:
        nilpotent = jnp.where(row // 8 == col // 8, -item[2], 0.0)
        firsts.append((nilpotent, product3(nilpotent, nilpotent, left)))
    inverses = []
    for nilpotent, squared in firsts:
        cubed = product3(nilpotent, squared, left)
        fourth = product3(squared, squared, left)
        inverses.append((unit + nilpotent + squared + cubed, fourth))
    inverses = [first + product3(first, fourth, left) for first, fourth in inverses]
    for size in (8, 16, 32):
        mask = (row // (2 * size) == col // (2 * size)) & (row // size != col // size)
        inner = [
            product3(jnp.where(mask, item[2], 0.0), inverse, left)
            for item, inverse in zip(work, inverses)
        ]
        inverses = [
            inverse - product3(inverse, middle, left) for inverse, middle in zip(inverses, inner)
        ]
    freshes = [product3(inverse, item[4], left) for item, inverse in zip(work, inverses)]
    for item, fresh in zip(work, freshes):
        lanes, key, _, attend, _, tail, head = item
        out = product3(attend, fresh, left)
        pattn[:, lanes] = gated(out, pg[:, lanes].astype(F32), gain)
        high, low = split2(fresh * tail)
        final = dot_tn(
            jnp.concatenate([key, key], axis=0),
            jnp.concatenate([high, low], axis=0).astype(BF16),
        )
        high, low = split2(final)
        state[head] = jnp.concatenate([high, low], axis=0).astype(BF16)


def sample_head(head, x2, aux, gain, state, o2):
    lanes = pl.ds(pl.multiple_of(head * 128, 128), 128)
    lane = iota((TOK, 128), 1)
    query, key = x2[pl.ds(0, 64), lanes], x2[pl.ds(64, 64), lanes]
    value = x2[pl.ds(128, 64), lanes].astype(F32)
    gate = x2[pl.ds(192, 64), lanes].astype(F32)
    both = jnp.concatenate([query, key], axis=0)
    seen = dot(jnp.concatenate([both, both], axis=1), state[head])
    query, key = query.astype(F32), key.astype(F32)
    query_norm = lax.rsqrt(jnp.sum(query * query, axis=-1, keepdims=True) + EPS)
    key_norm = lax.rsqrt(jnp.sum(key * key, axis=-1, keepdims=True) + EPS)
    query, key = query * query_norm, key * key_norm
    query_seen, key_seen = seen[:64] * query_norm, seen[64:] * key_norm
    beta = jnp.sum(jnp.where(lane == head, aux, 0.0), axis=-1, keepdims=True)
    decay = jnp.sum(jnp.where(lane == head + 16, aux, 0.0), axis=-1, keepdims=True)

    def step(array, index):
        return array[16 * index : 16 * index + 16]

    logs = [step(decay, 0)]
    for index in range(1, 4):
        logs.append(logs[-1] + step(decay, index))
    freshes, outs = [], []
    for now in range(4):
        start = jnp.exp(logs[now])
        recalled = start * step(key_seen, now)
        out = start * step(query_seen, now)
        for earlier in range(now):
            keep = jnp.exp(logs[now] - logs[earlier])
            past = step(key, earlier)
            key_inner = jnp.sum(step(key, now) * past, axis=-1, keepdims=True)
            query_inner = jnp.sum(step(query, now) * past, axis=-1, keepdims=True)
            recalled = recalled + (keep * key_inner) * freshes[earlier]
            out = out + (keep * query_inner) * freshes[earlier]
        fresh = step(beta, now) * (step(value, now) - recalled)
        own = jnp.sum(step(query, now) * step(key, now), axis=-1, keepdims=True)
        freshes.append(fresh)
        outs.append(out + own * fresh)
    o2[:, lanes] = gated(jnp.concatenate(outs, axis=0), gate, gain)


def recurrence_kernel(
    pq, pk, pv, pg, pbeta, pdecay, sq, sk, sv, sg, sbeta, sdecay, gain_ref,
    pattn, sattn,
    sendb, recvb, state, x2, aux_ref, o2, ret_send, ret_recv, log_rows, beta_rows,
    send_sem, recv_sem, send_sem2, recv_sem2,
):
    n = 16
    me = lax.axis_index("sample")

    def peer(index):
        return {"sample": index}

    barrier = pltpu.get_barrier_semaphore()

    def greet(i, carry):
        pl.semaphore_signal(barrier, inc=1, device_id=peer(lax.rem(me + i, n)), device_id_type=MESH)
        return carry

    lax.fori_loop(1, n, greet, 0)

    swap = swap_matrix()
    for tile in range(0, DIM, 256):
        lanes = pl.ds(tile, 256)
        rows = jnp.concatenate([ref[:, lanes] for ref in (sq, sk, sv, sg)], axis=0)
        sendb[:, :, lanes] = dot(swap, rows).astype(BF16).reshape(16, 16, 256)
    head_row, lane = iota((16, 128), 0), iota((16, 128), 1)
    put_beta = jnp.where(lane == head_row, 1.0, 0.0).astype(BF16)
    put_decay = jnp.where(lane == head_row + 16, 1.0, 0.0).astype(BF16)
    aux = (dot(sbeta[...], put_beta) + dot(sdecay[...], put_decay)).astype(BF16)
    aux = jnp.concatenate([aux, jnp.zeros((192, 128), BF16)], axis=0)
    sendb[:, :, pl.ds(DIM, 128)] = dot(swap, aux).astype(BF16).reshape(16, 16, 128)

    pl.semaphore_wait(barrier, n - 1)

    def outward(i):
        there = lax.rem(me + i, n)
        return pltpu.make_async_remote_copy(
            src_ref=sendb.at[there], dst_ref=recvb.at[me],
            send_sem=send_sem.at[i], recv_sem=recv_sem.at[i],
            device_id=peer(there), device_id_type=MESH,
        )

    def inward(i):
        there = lax.rem(me + n - i, n)
        return pltpu.make_async_remote_copy(
            src_ref=sendb.at[there], dst_ref=recvb.at[there],
            send_sem=send_sem.at[i], recv_sem=recv_sem.at[i],
            device_id=peer(there), device_id_type=MESH,
        )

    def back(i):
        there = lax.rem(me + i, n)
        return pltpu.make_async_remote_copy(
            src_ref=ret_send.at[there], dst_ref=ret_recv.at[me],
            send_sem=send_sem2.at[i], recv_sem=recv_sem2.at[i],
            device_id=peer(there), device_id_type=MESH,
        )

    def back_in(i):
        there = lax.rem(me + n - i, n)
        return pltpu.make_async_remote_copy(
            src_ref=ret_send.at[there], dst_ref=ret_recv.at[there],
            send_sem=send_sem2.at[i], recv_sem=recv_sem2.at[i],
            device_id=peer(there), device_id_type=MESH,
        )

    def each(action):
        def run(i, carry):
            action(i)
            return carry

        lax.fori_loop(1, n, run, 0)

    each(lambda i: outward(i).start())
    recvb[me] = sendb[me]

    token, later = iota((TOK, 128), 0), iota((TOK, 128), 1) % TOK
    ones = jnp.where(token <= later, 1.0, 0.0).astype(BF16)
    same = jnp.where(token == later, 1.0, 0.0).astype(BF16)
    log_rows[...] = dot_tn(pdecay[...], ones)
    beta_rows[...] = dot_tn(pbeta[...], same)
    gain = gain_ref[...]

    def prompt_group(group, carry):
        heads = [group * 4 + k for k in range(4)]
        prompt_heads(heads, pq, pk, pv, pg, gain, log_rows, beta_rows, state, pattn)
        return carry

    lax.fori_loop(0, 4, prompt_group, 0)

    each(lambda i: inward(i).wait_recv())
    for tile in range(0, DIM, 256):
        lanes = pl.ds(tile, 256)
        x2[:, lanes] = dot(swap, recvb[:, :, lanes].reshape(256, 256)).astype(BF16)
    aux_ref[...] = dot(swap[:64], recvb[:, :, pl.ds(DIM, 128)].reshape(256, 128))

    def sample_group(group, carry):
        aux = aux_ref[...]
        for k in range(2):
            sample_head(group * 2 + k, x2, aux, gain, state, o2)
        return carry

    lax.fori_loop(0, 8, sample_group, 0)

    rows = jnp.concatenate([o2[:, pl.ds(512 * c, 512)] for c in range(4)], axis=0)
    ret_send[...] = dot(swap, rows).astype(BF16).reshape(16, 16, 512)
    each(lambda i: back(i).start())
    ret_recv[me] = ret_send[me]
    each(lambda i: back_in(i).wait_recv())
    rows = dot(swap, ret_recv[...].reshape(256, 512)).astype(BF16)
    for c in range(4):
        sattn[:, pl.ds(512 * c, 512)] = rows[64 * c : 64 * c + 64]
    each(lambda i: outward(i).wait_send())
    each(lambda i: back(i).wait_send())


def recurrence(*args):
    vmem = pl.BlockSpec(memory_space=pltpu.VMEM)
    dma = pltpu.SemaphoreType.DMA((16,))
    return pl.pallas_call(
        recurrence_kernel,
        out_shape=[jax.ShapeDtypeStruct((TOK, DIM), BF16)] * 2,
        in_specs=[vmem] * len(args),
        out_specs=[vmem] * 2,
        scratch_shapes=[
            pltpu.VMEM((16, 16, WIDE), BF16),
            pltpu.VMEM((16, 16, WIDE), BF16),
            pltpu.VMEM((16, 256, 128), BF16),
            pltpu.VMEM((256, DIM), BF16),
            pltpu.VMEM((TOK, 128), F32),
            pltpu.VMEM((TOK, DIM), BF16),
            pltpu.VMEM((16, 16, 512), BF16),
            pltpu.VMEM((16, 16, 512), BF16),
            pltpu.VMEM((16, 128), F32),
            pltpu.VMEM((16, 128), F32),
            dma, dma, dma, dma,
        ],
        compiler_params=pltpu.CompilerParams(
            collective_id=0, has_side_effects=True, vmem_limit_bytes=48 * 2**20
        ),
        name="recurrence",
    )(*args)


SEMS = 22


class Batch:
    def __init__(self, rows, place, peers, bufs, send, recv):
        self.rows = rows
        self.y, self.zh, self.c = place
        self.zp, self.yu, self.yd, self.cp = peers
        (self.wide, self.part, self.cin, self.y1d, self.y1u, self.y2d, self.y2u, self.zin) = bufs
        self.send, self.recv = send, recv
        self.started = []

    def at_y(self, offset):
        return lax.rem(self.y + offset, 4)

    def copy(self, index, src, dst, peer):
        return pltpu.make_async_remote_copy(
            src_ref=src, dst_ref=dst, send_sem=self.send.at[index], recv_sem=self.recv.at[index],
            device_id={"expert": peer}, device_id_type=MESH,
        )

    def go(self, index, src, dst, peer):
        copy = self.copy(index, src, dst, peer)
        copy.start()
        self.started.append(copy)

    def arrived(self, index, dst):
        self.copy(index, dst, dst, self.cp).wait_recv()

    def slot(self, offset, zh):
        return self.c * 8 + self.at_y(offset) * 2 + zh

    def block(self, offset, zh):
        return self.wide.at[self.slot(offset, zh)]

    def pair(self, offset, c):
        return self.wide.at[pl.ds(c * 8 + self.at_y(offset) * 2, 2)]

    def spread_z(self):
        own = self.block(0, self.zh)
        self.go(0, own, own, self.zp)

    def spread_own(self):
        own = self.block(0, self.zh)
        self.go(1, own, own, self.yu)
        self.go(3, own, own, self.yd)

    def spread_other(self):
        other = self.block(0, 1 - self.zh)
        self.arrived(0, other)
        self.go(2, other, other, self.yu)
        self.go(4, other, other, self.yd)
        pair = self.pair(0, self.c)
        self.go(9, pair, pair, self.cp)

    def spread_relay(self):
        left, right = pl.ds(0, HALF), pl.ds(HALF, WIDE - HALF)
        for k, zh in enumerate((self.zh, 1 - self.zh)):
            block = self.block(3, zh)
            self.arrived(1 + k, block)
            part = block.at[:, left]
            self.go(5 + k, part, part, self.yu)
            block = self.block(1, zh)
            self.arrived(3 + k, block)
            part = block.at[:, right]
            self.go(7 + k, part, part, self.yd)
        for offset in (1, 3):
            pair = self.pair(offset, self.c)
            self.go(9 + offset, pair, pair, self.cp)

    def spread_far(self):
        left, right = pl.ds(0, HALF), pl.ds(HALF, WIDE - HALF)
        for k, zh in enumerate((self.zh, 1 - self.zh)):
            block = self.block(2, zh)
            self.arrived(5 + k, block.at[:, left])
            self.arrived(7 + k, block.at[:, right])
        pair = self.pair(2, self.c)
        self.go(11, pair, pair, self.cp)

    def spread_end(self):
        for offset in range(4):
            self.arrived(9 + offset, self.pair(offset, 1 - self.c))

    def sum_core(self):
        for offset in (2, 1, 3, 0):
            at = self.at_y(offset) * 2
            self.go(
                13 + offset,
                self.part.at[pl.ds((1 - self.c) * 8 + at, 2)],
                self.cin.at[pl.ds(at, 2)],
                self.cp,
            )

    def add_core(self, offset):
        at = self.at_y(offset) * 2
        self.arrived(13 + offset, self.cin.at[pl.ds(at, 2)])

    def sums(self, offset, lanes):
        at = self.at_y(offset) * 2
        return self.part[pl.ds(self.c * 8 + at, 2), :, lanes].astype(F32) + self.cin[
            pl.ds(at, 2), :, lanes
        ].astype(F32)

    def put(self, offset, lanes, value):
        at = self.at_y(offset) * 2
        self.part[pl.ds(self.c * 8 + at, 2), :, lanes] = value.astype(BF16)

    def tiles(self, body):
        width = 512 if self.rows == 16 else 256

        def run(i, carry):
            body(i * width, width)
            return carry

        lax.fori_loop(0, HALF // width, run, 0)

    def lanes(self, start, width):
        return pl.ds(pl.multiple_of(start, 256), width)

    def sum_first(self):
        self.add_core(2)

        def body(start, width):
            for base in (0, HALF):
                lanes = self.lanes(base + start, width)
                self.put(2, lanes, self.sums(2, lanes))

        self.tiles(body)
        ref = self.part.at[pl.ds(self.c * 8 + self.at_y(2) * 2, 2)]
        self.go(17, ref.at[:, :, pl.ds(0, HALF)], self.y1d, self.yu)
        self.go(18, ref.at[:, :, pl.ds(HALF, HALF)], self.y1u, self.yd)

    def sum_second(self):
        self.add_core(1)
        self.add_core(3)
        self.arrived(17, self.y1d)
        self.arrived(18, self.y1u)

        def body(start, width):
            near, far = self.lanes(start, width), self.lanes(HALF + start, width)
            self.put(1, near, self.sums(1, near) + self.y1d[:, :, near].astype(F32))
            self.put(1, far, self.sums(1, far))
            self.put(3, near, self.sums(3, near))
            self.put(3, far, self.sums(3, far) + self.y1u[:, :, near].astype(F32))

        self.tiles(body)
        ref = self.part.at[pl.ds(self.c * 8 + self.at_y(1) * 2, 2)]
        self.go(19, ref, self.y2d, self.yu)
        ref = self.part.at[pl.ds(self.c * 8 + self.at_y(3) * 2, 2)]
        self.go(20, ref, self.y2u, self.yd)

    def sum_third(self):
        self.add_core(0)
        self.arrived(19, self.y2d)
        self.arrived(20, self.y2u)

        def body(start, width):
            for base in (0, HALF):
                lanes = self.lanes(base + start, width)
                total = (
                    self.sums(0, lanes)
                    + self.y2d[:, :, lanes].astype(F32)
                    + self.y2u[:, :, lanes].astype(F32)
                )
                self.put(0, lanes, total)

        self.tiles(body)
        self.go(21, self.part.at[self.slot(0, 1 - self.zh)], self.zin, self.zp)

    def sum_end(self):
        self.arrived(21, self.zin)

    def total(self, lanes):
        return self.part[self.slot(0, self.zh), :, lanes].astype(F32) + self.zin[
            :, lanes
        ].astype(F32)

    def finish(self):
        for copy in self.started:
            copy.wait_send()


def expert_kernel(
    pin, pattn, proutes, pweights, sin, sattn, sroutes, sweights, gain_ref, wg_hbm, wu_hbm, wd_hbm,
    pout, sout,
    wg, wu, wd, hid, presid, sresid,
    pwide, ppart, pcin, py1d, py1u, py2d, py2u, pzin,
    dwide, dpart, dcin, dy1d, dy1u, dy2d, dy2u, dzin,
    send, recv, wsem,
):
    me = lax.axis_index("expert")
    y, zh, c = me // 4, (me // 2) % 2, me % 2
    zp = y * 4 + (1 - zh) * 2 + c
    yu = lax.rem(y + 1, 4) * 4 + zh * 2 + c
    yd = lax.rem(y + 3, 4) * 4 + zh * 2 + c
    cp = y * 4 + zh * 2 + (1 - c)
    barrier = pltpu.get_barrier_semaphore()
    for other in (zp, yu, yd, cp):
        pl.semaphore_signal(barrier, inc=1, device_id={"expert": other}, device_id_type=MESH)
    weights = [
        pltpu.make_async_copy(src, dst, wsem.at[i])
        for i, (src, dst) in enumerate(((wg_hbm, wg), (wu_hbm, wu), (wd_hbm, wd)))
    ]
    for copy in weights:
        copy.start()

    place, peers = (y, zh, c), (zp, yu, yd, cp)
    prompt = Batch(
        TOK, place, peers, (pwide, ppart, pcin, py1d, py1u, py2d, py2u, pzin), send.at[4], recv.at[4]
    )
    steps = [
        Batch(
            16, place, peers,
            tuple(ref.at[s] for ref in (dwide, dpart, dcin, dy1d, dy1u, dy2d, dy2u, dzin)),
            send.at[s], recv.at[s],
        )
        for s in range(4)
    ]
    gain = gain_ref[...]
    own = c * 8 + y * 2 + zh

    def weight_lanes(routes, values, rows):
        lane = iota((rows, 128), 1)
        table = jnp.zeros((rows, 128), F32)
        for k in range(10):
            table = table + jnp.where(lane % 16 == routes[:, k : k + 1], values[:, k : k + 1], 0.0)
        high, rest = split2(table)
        middle, low = split2(rest)
        table = jnp.where(lane < 16, high, jnp.where(lane < 32, middle, low))
        return jnp.where(lane < 48, table, 0.0).astype(BF16)

    def norm(resid):
        scaled = resid * lax.rsqrt(jnp.mean(resid * resid, axis=-1, keepdims=True) + EPS)
        return (scaled * gain).astype(BF16)

    def mlp(wide, part, rows, first, count):
        blocks = pl.ds(first, count)
        lane = iota((256, 128), 1)
        table = wide[blocks, :, pl.ds(DIM, 128)].reshape(256, 128).astype(F32)
        scale = jnp.sum(jnp.where(lane % 16 == me, table, 0.0), axis=-1, keepdims=True)

        def up(i, carry):
            lanes = pl.ds(pl.multiple_of(i * 256, 256), 256)
            x = wide[blocks, :, pl.ds(0, DIM)].reshape(256, DIM)
            hid[:, lanes] = (silu(dot(x, wg[:, lanes])) * dot(x, wu[:, lanes])).astype(BF16)
            return carry

        lax.fori_loop(0, FF // 256, up, 0)

        def down(i, carry):
            lanes = pl.ds(pl.multiple_of(i * 256, 256), 256)
            made = dot(hid[...], wd[:, lanes]).astype(BF16).astype(F32) * scale
            part[blocks, :, lanes] = made.astype(BF16).reshape(count, rows, 256)
            return carry

        lax.fori_loop(0, DIM // 256, down, 0)

    def prompt_mlp(first, last):
        def run(i, carry):
            mlp(pwide, ppart, TOK, i * 4, 4)
            return carry

        lax.fori_loop(first, last, run, 0)

    def open_prompt():
        for i in range(4):
            rows = pl.ds(16 * i, 16)
            resid = pin[rows, :].astype(F32) + pattn[rows, :].astype(F32)
            presid[rows, :] = resid
            pwide[own, rows, pl.ds(0, DIM)] = norm(resid)
        pwide[own, :, pl.ds(DIM, 128)] = weight_lanes(proutes[...], pweights[...], TOK)
        prompt.spread_z()

    def open_step(s):
        rows = pl.ds(16 * s, 16)
        resid = sin[rows, :].astype(F32) + sattn[rows, :].astype(F32)
        if s:
            resid = resid + sout[pl.ds(16 * s - 16, 16), :].astype(F32)
        sresid[...] = resid
        dwide[s, own, :, pl.ds(0, DIM)] = norm(resid)
        dwide[s, own, :, pl.ds(DIM, 128)] = weight_lanes(sroutes[rows, :], sweights[rows, :], 16)

    def close_step(s):
        everything = pl.ds(0, DIM)
        total = sresid[...] + steps[s].total(everything)
        sout[pl.ds(16 * s, 16), :] = total.astype(BF16)

    def nothing():
        pass

    def at_1_1():
        prompt.spread_other()

    def at_2_2():
        prompt.spread_end()
        prompt_mlp(0, 2)

    def at_2_3():
        prompt_mlp(2, 4)
        prompt.sum_core()

    points = [
        (open_prompt, prompt.spread_own, nothing),
        (prompt.spread_other, prompt.spread_relay, nothing),
        (prompt.spread_far, at_2_2, at_2_3),
        (prompt.sum_first, prompt.sum_second, prompt.sum_third),
    ]
    for s in range(4):
        step = steps[s]
        one, two, three = points[s]
        open_step(s)
        if s == 0:
            pl.semaphore_wait(barrier, 4)
        step.spread_z()
        step.spread_own()
        one()
        step.spread_other()
        step.spread_relay()
        step.spread_far()
        two()
        step.spread_end()
        if s == 0:
            for copy in weights:
                copy.wait()
        mlp(step.wide, step.part, 16, 0, 16)
        step.sum_core()
        step.sum_first()
        step.sum_second()
        three()
        step.sum_third()
        step.sum_end()
        close_step(s)
    prompt.sum_end()

    def last(i, carry):
        lanes = pl.ds(pl.multiple_of(i * 256, 256), 256)
        pout[:, lanes] = (presid[:, lanes] + prompt.total(lanes)).astype(BF16)
        return carry

    lax.fori_loop(0, DIM // 256, last, 0)
    for batch in steps + [prompt]:
        batch.finish()


def experts(*args):
    vmem = pl.BlockSpec(memory_space=pltpu.VMEM)
    anywhere = pl.BlockSpec(memory_space=pl.ANY)

    def buffers(lead, rows):
        shapes = [
            (16, rows, WIDE), (16, rows, DIM), (8, rows, DIM), (2, rows, HALF), (2, rows, HALF),
            (2, rows, DIM), (2, rows, DIM), (rows, DIM),
        ]
        return [pltpu.VMEM(lead + shape, BF16) for shape in shapes]

    return pl.pallas_call(
        expert_kernel,
        out_shape=[jax.ShapeDtypeStruct((TOK, DIM), BF16)] * 2,
        in_specs=[vmem] * 9 + [anywhere] * 3,
        out_specs=[vmem] * 2,
        scratch_shapes=[
            pltpu.VMEM((DIM, FF), BF16),
            pltpu.VMEM((DIM, FF), BF16),
            pltpu.VMEM((FF, DIM), BF16),
            pltpu.VMEM((256, FF), BF16),
            pltpu.VMEM((TOK, DIM), F32),
            pltpu.VMEM((16, DIM), F32),
            *buffers((), TOK),
            *buffers((4,), 16),
            pltpu.SemaphoreType.DMA((5, SEMS)),
            pltpu.SemaphoreType.DMA((5, SEMS)),
            pltpu.SemaphoreType.DMA((3,)),
        ],
        compiler_params=pltpu.CompilerParams(
            collective_id=1, has_side_effects=True, vmem_limit_bytes=56 * 2**20
        ),
        name="experts",
    )(*args)


def body(
    prompt_input, prompt_query, prompt_key, prompt_value, prompt_gate, prompt_beta, prompt_decay,
    prompt_routes, prompt_weights, sample_input, sample_query, sample_key, sample_value,
    sample_gate, sample_beta, sample_decay, sample_routes, sample_weights, head_gain, norm_gain,
    expert_gate, expert_up, expert_down,
):
    def rows(array):
        return array.reshape(TOK, array.shape[-1])

    prompt_attn, sample_attn = recurrence(
        rows(prompt_query), rows(prompt_key), rows(prompt_value), rows(prompt_gate),
        rows(prompt_beta), rows(prompt_decay),
        rows(sample_query), rows(sample_key), rows(sample_value), rows(sample_gate),
        rows(sample_beta), rows(sample_decay), head_gain[None],
    )
    prompt_output, sample_output = experts(
        rows(prompt_input), prompt_attn, rows(prompt_routes), rows(prompt_weights),
        rows(sample_input), sample_attn, rows(sample_routes), rows(sample_weights),
        norm_gain[None], expert_gate[0], expert_up[0], expert_down[0],
    )
    return prompt_output.reshape(prompt_input.shape), sample_output.reshape(sample_input.shape)


def solution(mesh):
    by_prompt = P("expert", "sample", None, None)
    by_sample = P(None, "sample", "expert", None, None)
    by_expert = P("expert", None, None)
    return jax.shard_map(
        body,
        mesh=mesh,
        in_specs=(by_prompt,) * 9 + (by_sample,) * 9 + (P(), P()) + (by_expert,) * 3,
        out_specs=(by_prompt, by_sample),
        check_vma=False,
    )
```
